32 devices in a mesh: head: 4 (over x, core), seq: 8 (over z, y).
Axes of the slice: x: 2, y: 2, z: 4, core: 2. Of those that a mesh axis runs over, the one named last changes fastest.
Arguments:
- tokens: bfloat16 [1536, 2304], P('seq'), may hold values from -70 to 70
- cotangent: bfloat16 [3, 1536, 2304], P(None, 'seq'), may hold values from -6 to 6
- doc_lengths: int32 [8], replicated, may hold values from 1 to 1344, as said below
- pad_mask: int32 [1536], P('seq'), may hold values 0 or 1
- gain_attn_in: float32 [2304], replicated, may hold values from 1.2 to 1.8
- gain_attn_out: float32 [2304], replicated, may hold values from 0.1 to 1.9
- gain_mlp_in: float32 [2304], replicated, may hold values from 0.1 to 1.9
- gain_mlp_out: float32 [2304], replicated, may hold values from 0.1 to 1.9
- w_query: bfloat16 [2048, 2304], P('head'), may hold values from -128 to 128
- w_key: bfloat16 [1024, 2304], P('head'), may hold values from -128 to 128
- w_value: bfloat16 [1024, 2304], P('head'), may hold values from -128 to 128
- w_out: bfloat16 [2048, 2304], P('head'), may hold values from -128 to 128
- w_gate: bfloat16 [9216, 2304], P('head'), may hold values from -128 to 128
- w_up: bfloat16 [9216, 2304], P('head'), may hold values from -128 to 128
- w_down: bfloat16 [9216, 2304], P('head'), may hold values from -128 to 128
Outputs:
- activations: bfloat16 [3, 1536, 2304], P(None, 'seq')
- grad_tokens: bfloat16 [1536, 2304], P('seq')
- grad_w_query: float32 [2048, 2304], P(('head', 'seq'))
- grad_w_key: float32 [1024, 2304], P(('head', 'seq'))
- grad_w_value: float32 [1024, 2304], P(('head', 'seq'))
- grad_w_out: float32 [2048, 2304], P(('head', 'seq'))
- grad_w_gate: float32 [9216, 2304], P(('head', 'seq'))
- grad_w_up: float32 [9216, 2304], P(('head', 'seq'))
- grad_w_down: float32 [9216, 2304], P(('head', 'seq'))
- grad_gain_attn_in: float32 [2304], P('seq')
- grad_gain_attn_out: float32 [2304], P('seq')
- grad_gain_mlp_in: float32 [2304], P('seq')
- grad_gain_mlp_out: float32 [2304], P('seq')
The draws below stay inside these ranges and needn't reach their ends.
Inputs may be any that keep to these rules, and one draw needn't show every extreme that they name: `doc_lengths`: the lengths sum to 1536; exactly one document, neither the first nor the last, has length 1344, and the others share 192 tokens.
All inputs are finite; a program needn't handle non-finite values. No bound on the sum of `pad_mask` on one device may be relied on, other than what follows from the above.
Results may differ from the reference program's by a relative error of at most 0.028.
Values may be sent and summed in bfloat16 or wider, within the bound.
No kernel may reach another device: no remote copies, remote signals or barrier semaphores. Data moves between devices by JAX's collectives and lax.ppermute only.
A program may use at most 320 MiB of HBM per device.

```python
import math
import jax
import jax.numpy as jnp
from jax import lax

D = 2304
H = 8
KVH = 4
HD = 256
FF = 9216
SOFTCAP = 50
NDOC = 8
TOK_DEV = 192
SEQ_LEN = 1536


def draw_tokens(key, part):
    key = jax.random.fold_in(key, 5)
    key_base, key_row, key_col = jax.random.split(key, 3)
    base = jnp.clip(jax.random.normal(key_base, (SEQ_LEN, D), jnp.float32), -4.0, 4.0)
    spread = 10.0
    row_scale = jnp.exp(jax.random.uniform(key_row, (SEQ_LEN, 1), jnp.float32, -0.5, 0.5) * math.log(spread))
    col_scale = jnp.exp(jax.random.uniform(key_col, (1, D), jnp.float32, -0.5, 0.5) * math.log(spread))
    return (base * row_scale * col_scale).astype(jnp.bfloat16)


def draw_doc_lengths(key, part):
    key = jax.random.fold_in(key, 11)
    key_cut, key_place = jax.random.split(key)
    picked = jax.random.permutation(key_cut, TOK_DEV - 1)[:NDOC - 2] + 1
    cuts = jnp.sort(picked.astype(jnp.int32))
    edges = jnp.concatenate([jnp.zeros((1,), jnp.int32), cuts, jnp.full((1,), TOK_DEV, jnp.int32)])
    short_lengths = edges[1:] - edges[:-1]
    place = jax.random.randint(key_place, (), 1, NDOC - 1)
    slots = jnp.arange(NDOC, dtype=jnp.int32)
    earlier = short_lengths[jnp.clip(slots, 0, NDOC - 2)]
    later = short_lengths[jnp.clip(slots - 1, 0, NDOC - 2)]
    lengths = jnp.where(slots < place, earlier, jnp.where(slots == place, SEQ_LEN - TOK_DEV, later))
    return lengths.astype(jnp.int32)


def plant(values, stream_key, least, largest):
    extent = values.shape
    spot = [jax.random.randint(jax.random.fold_in(stream_key, axis), (), 0, extent[axis]) for axis in range(len(extent))]
    values = values.at[tuple(spot)].set(least)
    longest = extent.index(max(extent))
    spot[longest] = (spot[longest] + 1) % extent[longest]
    return values.at[tuple(spot)].set(largest)


def block_scale(stream_key, shape, cuts, least, top_value):
    def one(dim, shards_of):
        heights = jax.random.uniform(jax.random.fold_in(jax.random.fold_in(stream_key, 6), dim), (shards_of,), jnp.float32, least / len(cuts), top_value / len(cuts))
        return jnp.repeat(jnp.exp(heights), shape[dim] // shards_of).reshape((-1,) + (1,) * (len(shape) - dim - 1))

    level = one(*cuts[0])
    for cut in cuts[1:]:
        level = level * one(*cut)
    return level


def scatter_about(rng, shape, width, reach, shards=(), kind=jnp.bfloat16):
    level = block_scale(rng, shape, shards, -0.22, 0.18) if shards else 1.0
    array = jax.random.normal(rng, shape, jnp.float32) * width * level
    return jnp.minimum(jnp.maximum(array, -reach), reach).astype(kind)


def setup_inputs(seed: int = 0) -> dict:
    streams_of = jax.random.split(jax.random.key(seed), 16)
    tokens = draw_tokens(jax.random.fold_in(streams_of[15], 71), 0)
    cotangent = scatter_about(streams_of[1], (3, SEQ_LEN, D), 1.0, 6.0, ((1, 8),))
    doc_lengths = draw_doc_lengths(jax.random.fold_in(streams_of[15], 71), 0)
    pad_mask = plant((jax.random.randint(streams_of[3], (SEQ_LEN,), 0, 8) < 7).astype(jnp.int32), jax.random.fold_in(streams_of[3], 1), 0, 1)
    gain_attn_in = jnp.clip(jnp.exp(jax.random.uniform(streams_of[4], (D,), jnp.float32, math.log(1.2), math.log(1.8))), 1.2, 1.8)
    gain_attn_out = jnp.clip(1.0 + 0.18 * jax.random.normal(streams_of[5], (D,), jnp.float32), 0.1, 1.9)
    gain_mlp_in = jnp.clip(1.0 + 0.18 * jax.random.normal(streams_of[6], (D,), jnp.float32), 0.1, 1.9)
    gain_mlp_out = jnp.clip(1.0 + 0.18 * jax.random.normal(streams_of[7], (D,), jnp.float32), 0.1, 1.9)
    w_query = jnp.clip(jax.random.uniform(streams_of[8], (H * HD, D), jnp.float32, -128.0, 128.0) * block_scale(streams_of[8], (H * HD, D), ((0, 4),), -0.4, 0.0), -128.0, 128.0).astype(jnp.bfloat16)
    w_key = jnp.clip(jax.random.uniform(streams_of[9], (KVH * HD, D), jnp.float32, -128.0, 128.0) * block_scale(streams_of[9], (KVH * HD, D), ((0, 4),), -0.4, 0.0), -128.0, 128.0).astype(jnp.bfloat16)
    w_value = jnp.clip(jax.random.uniform(streams_of[10], (KVH * HD, D), jnp.float32, -128.0, 128.0) * block_scale(streams_of[10], (KVH * HD, D), ((0, 4),), -0.4, 0.0), -128.0, 128.0).astype(jnp.bfloat16)
    w_out = jnp.clip(jax.random.uniform(streams_of[11], (H * HD, D), jnp.float32, -128.0, 128.0) * block_scale(streams_of[11], (H * HD, D), ((0, 4),), -0.4, 0.0), -128.0, 128.0).astype(jnp.bfloat16)
    w_gate = jnp.clip(jax.random.uniform(streams_of[12], (FF, D), jnp.float32, -128.0, 128.0) * block_scale(streams_of[12], (FF, D), ((0, 4),), -0.4, 0.0), -128.0, 128.0).astype(jnp.bfloat16)
    w_up = jnp.clip(jax.random.uniform(streams_of[13], (FF, D), jnp.float32, -128.0, 128.0) * block_scale(streams_of[13], (FF, D), ((0, 4),), -0.4, 0.0), -128.0, 128.0).astype(jnp.bfloat16)
    w_down = jnp.clip(jax.random.uniform(streams_of[14], (FF, D), jnp.float32, -128.0, 128.0) * block_scale(streams_of[14], (FF, D), ((0, 4),), -0.4, 0.0), -128.0, 128.0).astype(jnp.bfloat16)
    return {"tokens": tokens, "cotangent": cotangent, "doc_lengths": doc_lengths, "pad_mask": pad_mask, "gain_attn_in": gain_attn_in, "gain_attn_out": gain_attn_out, "gain_mlp_in": gain_mlp_in, "gain_mlp_out": gain_mlp_out, "w_query": w_query, "w_key": w_key, "w_value": w_value, "w_out": w_out, "w_gate": w_gate, "w_up": w_up, "w_down": w_down}


@jax.custom_vjp
def low(v):
    return lax.optimization_barrier(v.astype(jnp.bfloat16)).astype(jnp.float32)

@jax.custom_vjp
def low_back(v):
    return v

def low_keep(v):
    return (low(v), None)

def low_pass(kept, grad):
    return (grad,)

def back_keep(v):
    return (v, None)

def back_low(kept, grad):
    return (low(grad),)
low.defvjp(low_keep, low_pass)
low_back.defvjp(back_keep, back_low)

def matmul(left, right):
    return jnp.dot(left, right, precision=lax.Precision.HIGHEST)

def slice_codes(master, width_bits):
    whole = jnp.clip(jnp.floor(master) + 128.0, 0.0, 255.0)
    if width_bits == 8:
        return whole - 128.0
    step = 2.0 ** (8 - width_bits)
    return jnp.floor(whole / step) * step + step / 2.0 - 128.0

def rms_norm(value, gain):
    return value * lax.rsqrt(lax.optimization_barrier(jnp.mean(value * value, axis=-1, keepdims=True)) + 1e-06) * gain

def rotate(value, cosine, sine):
    half = value.shape[-1] // 2
    first = value[..., :half]
    second = value[..., half:]
    return jnp.concatenate([first * cosine - second * sine, second * cosine + first * sine], axis=-1)

def doc_info(positions, doc_lengths):
    ends = jnp.cumsum(doc_lengths).astype(jnp.int32)
    before = ends[None, :] <= positions[:, None]
    segment = lax.optimization_barrier(jnp.sum(before.astype(jnp.int32), axis=1)).astype(jnp.int32)
    offset = lax.optimization_barrier(jnp.sum(jnp.where(before, doc_lengths[None, :], 0), axis=1)).astype(jnp.int32)
    return (segment, (positions - offset).astype(jnp.int32))

def rope_tables(relative):
    freq = jnp.exp(jnp.arange(HD // 2, dtype=jnp.float32) * (-2.0 * math.log(10000.0) / HD))
    angle = relative.astype(jnp.float32)[:, None] * freq[None, :]
    return (jnp.cos(angle), jnp.sin(angle))

def block_forward(inputs, gains, weights, cosine, sine, segment, positions, pad_mask):
    gain_one, gain_two, gain_three, gain_four = gains
    code_query, code_key, code_value, code_out, code_gate, code_up, code_down = weights
    scale_model = 1.0 / (64.0 * math.sqrt(D))
    scale_heads = 1.0 / (64.0 * math.sqrt(H * HD))
    scale_hidden = 1.0 / (64.0 * math.sqrt(FF))
    length = inputs.shape[0]
    normed = low(low_back(rms_norm(inputs, gain_one)))
    query_raw = low_back(matmul(normed, code_query.T) * scale_model).reshape(length, H, HD)
    query = low(low_back(rotate(query_raw, cosine[:, None, :], sine[:, None, :])))
    key_raw = low_back(matmul(normed, code_key.T) * scale_model).reshape(length, KVH, HD)
    keys = low(low_back(rotate(key_raw, cosine[:, None, :], sine[:, None, :])))
    values = low(low_back(matmul(normed, code_value.T) * scale_model)).reshape(length, KVH, HD)
    keys = jnp.repeat(keys, H // KVH, axis=1)
    values = jnp.repeat(values, H // KVH, axis=1)
    block = min(256, length)
    count = length // block

    def attend(pieces):
        query_block, query_pos, query_seg = pieces
        raw_score = low_back(jnp.einsum('qhd,khd->hqk', query_block, keys, precision=lax.Precision.HIGHEST))
        capped = SOFTCAP * jnp.tanh(raw_score / (math.sqrt(HD) * SOFTCAP))
        allowed = (query_seg[:, None] == segment[None, :]) & (positions[None, :] <= query_pos[:, None])
        allowed = allowed & ((pad_mask[None, :] == 1) | (positions[None, :] == query_pos[:, None]))
        masked = jnp.where(allowed[None], capped, -1e+30)
        peak = lax.optimization_barrier(jnp.max(masked, axis=-1, keepdims=True))
        expo = jnp.where(allowed[None], jnp.exp(masked - peak), 0.0)
        probs = low(expo / lax.optimization_barrier(jnp.sum(expo, axis=-1, keepdims=True)))
        return jnp.einsum('hqk,khd->qhd', probs, values, precision=lax.Precision.HIGHEST)
    context = lax.map(jax.checkpoint(attend), (query.reshape(count, block, H, HD), positions.reshape(count, block), segment.reshape(count, block)))
    context = low(low_back(context.reshape(length, H * HD)))
    attn_out = low_back(matmul(context, code_out) * scale_heads)
    middle = inputs + rms_norm(attn_out, gain_two)
    normed_two = low(low_back(rms_norm(middle, gain_three)))
    gate_act = low_back(matmul(normed_two, code_gate.T) * scale_model)
    up_act = low_back(matmul(normed_two, code_up.T) * scale_model)
    hidden = low(low_back(jax.nn.gelu(gate_act, approximate=True) * up_act))
    feed_out = low_back(matmul(hidden, code_down) * scale_hidden)
    return middle + rms_norm(feed_out, gain_four)

def reference(tokens, cotangent, doc_lengths, pad_mask, gain_attn_in, gain_attn_out, gain_mlp_in, gain_mlp_out, w_query, w_key, w_value, w_out, w_gate, w_up, w_down):
    positions = jnp.arange(SEQ_LEN, dtype=jnp.int32)
    segment, relative = doc_info(positions, doc_lengths)
    cosine, sine = rope_tables(relative)
    inputs = tokens.astype(jnp.float32)
    gains = (gain_attn_in.astype(jnp.float32), gain_attn_out.astype(jnp.float32), gain_mlp_in.astype(jnp.float32), gain_mlp_out.astype(jnp.float32))
    masters = tuple((weight.astype(jnp.float32) for weight in (w_query, w_key, w_value, w_out, w_gate, w_up, w_down)))
    outputs = []
    grad_inputs = jnp.zeros_like(inputs)
    grad_gains = tuple((jnp.zeros_like(gain) for gain in gains))
    grad_weights = tuple((jnp.zeros_like(master) for master in masters))
    for width_index, width_bits in enumerate((8, 4, 2)):
        weights = tuple((slice_codes(master, width_bits) for master in masters))

        def width_layer(inputs_now, gains_now, weights_now):
            return block_forward(inputs_now, gains_now, weights_now, cosine, sine, segment, positions, pad_mask)
        result, pull = jax.vjp(width_layer, inputs, gains, weights)
        grad_in, grad_gain, grad_weight = pull(cotangent[width_index].astype(jnp.float32))
        outputs.append(result.astype(jnp.bfloat16))
        grad_inputs = grad_inputs + grad_in
        grad_gains = tuple((total + part for total, part in zip(grad_gains, grad_gain)))
        grad_weights = tuple((total + part for total, part in zip(grad_weights, grad_weight)))
    return (jnp.stack(outputs), grad_inputs.astype(jnp.bfloat16), grad_weights[0], grad_weights[1], grad_weights[2], grad_weights[3], grad_weights[4], grad_weights[5], grad_weights[6], grad_gains[0], grad_gains[1], grad_gains[2], grad_gains[3])
```

```python
import math

import jax
import jax.numpy as jnp
from jax import lax
from jax.sharding import PartitionSpec as P

D = 2304
H = 8
HD = 256
FF = 9216
SOFTCAP = 50


NEG_LARGE = -1e30


def for_sending(value):

    def short(part):
        return part.astype(jnp.bfloat16) if part.dtype == jnp.float32 else part

    return jax.tree.map(short, value)


def slice_codes(master, width_bits):
    whole = jnp.clip(jnp.floor(master.astype(jnp.float32)) + 128.0, 0.0, 255.0)
    if width_bits == 8:
        return (whole - 128.0).astype(jnp.bfloat16)
    step = 2.0 ** (8 - width_bits)
    return (jnp.floor(whole / step) * step + step / 2.0 - 128.0).astype(jnp.bfloat16)


def rms_norm(value, gain):
    return value * lax.rsqrt(jnp.mean(value * value, axis=-1, keepdims=True) + 1e-06) * gain


def rotate(value, cosine, sine):
    half = value.shape[-1] // 2
    first = value[..., :half]
    second = value[..., half:]
    return jnp.concatenate(
        [first * cosine - second * sine, second * cosine + first * sine], axis=-1
    )


def doc_info(positions, doc_lengths):
    slots = jnp.arange(doc_lengths.shape[0], dtype=jnp.int32)
    ends = jnp.sum(jnp.where(slots[:, None] <= slots[None, :], doc_lengths[:, None], 0), axis=0)
    before = ends[None, :] <= positions[:, None]
    segment = jnp.sum(before.astype(jnp.int32), axis=1)
    offset = jnp.sum(jnp.where(before, doc_lengths[None, :], 0), axis=1)
    return (segment, positions - offset)


def rope_tables(relative):
    freq = jnp.exp(jnp.arange(HD // 2, dtype=jnp.float32) * (-2.0 * math.log(10000.0) / HD))
    angle = relative.astype(jnp.float32)[:, None] * freq[None, :]
    return (jnp.cos(angle), jnp.sin(angle))


def times_rows(left, right):
    return lax.dot_general(
        left, right, (((1,), (1,)), ((), ())), preferred_element_type=jnp.float32
    )


def times_cols(left, right):
    return lax.dot_general(
        left, right, (((0,), (0,)), ((), ())), preferred_element_type=jnp.float32
    )


def product(left, right):
    return jnp.dot(left, right, preferred_element_type=jnp.float32)


def geglu(gate_act, up_act):
    return jax.nn.gelu(gate_act, approximate=True) * up_act


def body(
    tokens,
    cotangent,
    doc_lengths,
    pad_mask,
    gain_attn_in,
    gain_attn_out,
    gain_mlp_in,
    gain_mlp_out,
    w_query,
    w_key,
    w_value,
    w_out,
    w_gate,
    w_up,
    w_down,
):
    row_count = tokens.shape[0]
    positions = lax.axis_index("seq") * row_count + jnp.arange(row_count, dtype=jnp.int32)
    segment, relative = doc_info(positions, doc_lengths)
    cosine, sine = rope_tables(relative)
    cosine = cosine[:, None, :]
    sine = sine[:, None, :]
    group = w_query.shape[0] // HD
    query_pos = jnp.repeat(positions, group)
    query_seg = jnp.repeat(segment, group)
    scale_model = 1.0 / (64.0 * math.sqrt(D))
    scale_heads = 1.0 / (64.0 * math.sqrt(H * HD))
    scale_hidden = 1.0 / (64.0 * math.sqrt(FF))
    root_scale = 1.0 / math.sqrt(HD)
    inputs = tokens.astype(jnp.float32)

    def permitted(key_count, key_valid):
        key_pos = jnp.arange(key_count, dtype=jnp.int32)
        key_seg, _ = doc_info(key_pos, doc_lengths)
        allowed = (query_seg[:, None] == key_seg[None, :]) & (
            key_pos[None, :] <= query_pos[:, None]
        )
        return allowed & ((key_valid[None, :] == 1) | (key_pos[None, :] == query_pos[:, None]))

    outputs = []
    grad_inputs = jnp.zeros_like(inputs)
    totals = None
    for width_index, width_bits in enumerate((8, 4, 2)):
        code_query = slice_codes(w_query, width_bits)
        code_key = slice_codes(w_key, width_bits)
        code_value = slice_codes(w_value, width_bits)
        code_out = slice_codes(w_out, width_bits)
        code_gate = slice_codes(w_gate, width_bits)
        code_up = slice_codes(w_up, width_bits)
        code_down = slice_codes(w_down, width_bits)
        normed, pull_one = jax.vjp(rms_norm, inputs, gain_attn_in)
        normed_b = normed.astype(jnp.bfloat16)
        query_raw = (scale_model * times_rows(normed_b, code_query)).reshape(row_count, group, HD)
        query_flat = (
            rotate(query_raw, cosine, sine).astype(jnp.bfloat16).reshape(row_count * group, HD)
        )
        key_raw = (scale_model * times_rows(normed_b, code_key)).reshape(row_count, 1, HD)
        key_b = rotate(key_raw, cosine, sine).astype(jnp.bfloat16).reshape(row_count, HD)
        value_b = (scale_model * times_rows(normed_b, code_value)).astype(jnp.bfloat16)
        run_peak = jnp.full((row_count * group,), NEG_LARGE, jnp.float32)
        key_piece = lax.all_gather(key_b, "seq", axis=0, tiled=True)
        value_piece = lax.all_gather(value_b, "seq", axis=0, tiled=True)
        attend_key_valid = lax.all_gather(pad_mask, "seq", axis=0, tiled=True)
        attend_allowed = permitted(key_piece.shape[0], attend_key_valid)
        raw_score = times_rows(query_flat, key_piece)
        masked = jnp.where(
            attend_allowed, SOFTCAP * jnp.tanh(raw_score * (root_scale / SOFTCAP)), NEG_LARGE
        )
        new_peak = jnp.maximum(run_peak, jnp.max(masked, axis=1))
        expo = jnp.where(attend_allowed, jnp.exp(masked - new_peak[:, None]), 0.0)
        run_total = jnp.sum(expo, axis=1)
        run_acc = product(expo.astype(jnp.bfloat16), value_piece)
        run_peak, run_total, run_acc = (new_peak, run_total, run_acc)
        context = run_acc / run_total[:, None]
        log_total = run_peak + jnp.log(run_total)
        context_b = context.astype(jnp.bfloat16).reshape(row_count, group * HD)
        attn_out = lax.psum(
            (scale_heads * product(context_b, code_out)).astype(jnp.bfloat16), "head"
        ).astype(jnp.float32)
        branch_attn, pull_two = jax.vjp(rms_norm, attn_out, gain_attn_out)
        middle = inputs + branch_attn
        normed_two, pull_three = jax.vjp(rms_norm, middle, gain_mlp_in)
        normed_two_b = normed_two.astype(jnp.bfloat16)
        gate_act = scale_model * times_rows(normed_two_b, code_gate)
        up_act = scale_model * times_rows(normed_two_b, code_up)
        hidden, pull_glu = jax.vjp(geglu, gate_act, up_act)
        hidden_b = hidden.astype(jnp.bfloat16)
        feed_out = lax.psum(
            (scale_hidden * product(hidden_b, code_down)).astype(jnp.bfloat16), "head"
        ).astype(jnp.float32)
        branch_feed, pull_four = jax.vjp(rms_norm, feed_out, gain_mlp_out)
        outputs.append((middle + branch_feed).astype(jnp.bfloat16))
        grad_out = cotangent[width_index].astype(jnp.float32)
        grad_feed, grad_gain_four = pull_four(grad_out)
        grad_feed_b = grad_feed.astype(jnp.bfloat16)
        grad_hidden = scale_hidden * times_rows(grad_feed_b, code_down)
        term_down = scale_hidden * times_cols(hidden_b, grad_feed_b)
        grad_gate, grad_up = pull_glu(grad_hidden.astype(jnp.bfloat16).astype(jnp.float32))
        grad_gate_b = grad_gate.astype(jnp.bfloat16)
        grad_up_b = grad_up.astype(jnp.bfloat16)
        term_gate = scale_model * times_cols(grad_gate_b, normed_two_b)
        term_up = scale_model * times_cols(grad_up_b, normed_two_b)
        grad_normed_two = lax.psum(
            (scale_model * (product(grad_gate_b, code_gate) + product(grad_up_b, code_up))).astype(
                jnp.bfloat16
            ),
            "head",
        )
        grad_middle_norm, grad_gain_three = pull_three(grad_normed_two.astype(jnp.float32))
        grad_middle = grad_out + grad_middle_norm
        grad_attn, grad_gain_two = pull_two(grad_middle)
        grad_attn_b = grad_attn.astype(jnp.bfloat16)
        grad_context = scale_heads * times_rows(grad_attn_b, code_out)
        term_out = scale_heads * times_cols(context_b, grad_attn_b)
        grad_context_b = grad_context.astype(jnp.bfloat16).reshape(row_count * group, HD)
        row_delta = jnp.sum(grad_context_b.astype(jnp.float32) * context, axis=1)

        def attend_back(piece):
            key_piece, value_piece, key_valid = piece
            key_count = key_piece.shape[0]
            allowed = permitted(key_count, key_valid)
            raw_score = times_rows(query_flat, key_piece)
            bend_score = jnp.tanh(raw_score * (root_scale / SOFTCAP))
            masked = jnp.where(allowed, SOFTCAP * bend_score, NEG_LARGE)
            prob_full = jnp.where(allowed, jnp.exp(masked - log_total[:, None]), 0.0)
            grad_prob = times_rows(grad_context_b, value_piece)
            grad_raw = (
                prob_full
                * (grad_prob - row_delta[:, None])
                * (1.0 - bend_score * bend_score)
                * root_scale
            ).astype(jnp.bfloat16)
            grad_query = product(grad_raw, key_piece)
            key_term = times_cols(grad_raw, query_flat)
            value_term = times_cols(prob_full.astype(jnp.bfloat16), grad_context_b)
            return (grad_query, key_term, value_term)

        grad_query, grad_keys, grad_values = attend_back(
            (
                lax.all_gather(key_b, "seq", axis=0, tiled=True),
                lax.all_gather(value_b, "seq", axis=0, tiled=True),
                lax.all_gather(pad_mask, "seq", axis=0, tiled=True),
            )
        )
        key_sums = (
            lax.psum_scatter(
                grad_keys.astype(jnp.bfloat16), "seq", scatter_dimension=0, tiled=True
            ).astype(jnp.float32),
            lax.psum_scatter(
                grad_values.astype(jnp.bfloat16), "seq", scatter_dimension=0, tiled=True
            ).astype(jnp.float32),
        )
        grad_query_rot = (
            grad_query.astype(jnp.bfloat16).astype(jnp.float32).reshape(row_count, group, HD)
        )
        grad_query_b = (
            rotate(grad_query_rot, cosine, -sine)
            .astype(jnp.bfloat16)
            .reshape(row_count, group * HD)
        )
        grad_key_rot = (
            key_sums[0].astype(jnp.bfloat16).astype(jnp.float32).reshape(row_count, 1, HD)
        )
        grad_key_b = rotate(grad_key_rot, cosine, -sine).astype(jnp.bfloat16).reshape(row_count, HD)
        grad_value_b = key_sums[1].astype(jnp.bfloat16)
        term_query = scale_model * times_cols(grad_query_b, normed_b)
        term_key = scale_model * times_cols(grad_key_b, normed_b)
        term_value = scale_model * times_cols(grad_value_b, normed_b)
        partial_normed = scale_model * (
            product(grad_query_b, code_query)
            + product(grad_key_b, code_key)
            + product(grad_value_b, code_value)
        )
        grad_normed = lax.psum(partial_normed.astype(jnp.bfloat16), "head")
        grad_input_norm, grad_gain_one = pull_one(grad_normed.astype(jnp.float32))
        grad_inputs = grad_inputs + grad_middle + grad_input_norm
        new_terms = (
            term_query,
            term_key,
            term_value,
            term_out,
            term_gate,
            term_up,
            term_down,
            grad_gain_one,
            grad_gain_two,
            grad_gain_three,
            grad_gain_four,
        )
        if totals is None:
            totals = new_terms
        else:
            totals = jax.tree.map(lambda older, newer: older + newer, totals, new_terms)
    totals = jax.tree.map(
        lambda part: part.astype(jnp.float32),
        lax.psum_scatter(for_sending(totals), "seq", scatter_dimension=0, tiled=True),
    )
    return (
        jnp.stack(outputs),
        grad_inputs.astype(jnp.bfloat16),
        totals[0],
        totals[1],
        totals[2],
        totals[3],
        totals[4],
        totals[5],
        totals[6],
        totals[7],
        totals[8],
        totals[9],
        totals[10],
    )


def solution(mesh):
    in_specs = (
        P("seq", None),
        P(None, "seq", None),
        P(),
        P("seq"),
        P(),
        P(),
        P(),
        P(),
        P("head", None),
        P("head", None),
        P("head", None),
        P("head", None),
        P("head", None),
        P("head", None),
        P("head", None),
    )
    out_specs = (
        P(None, "seq", None),
        P("seq", None),
        P(("head", "seq"), None),
        P(("head", "seq"), None),
        P(("head", "seq"), None),
        P(("head", "seq"), None),
        P(("head", "seq"), None),
        P(("head", "seq"), None),
        P(("head", "seq"), None),
        P("seq"),
        P("seq"),
        P("seq"),
        P("seq"),
    )
    return jax.shard_map(body, mesh=mesh, in_specs=in_specs, out_specs=out_specs, check_vma=False)
```

```python
import math

import jax
import jax.numpy as jnp
from jax import lax
from jax.sharding import PartitionSpec as P

HD = 256
SOFTCAP = 50.0
WIDTHS = (8, 4, 2)
GROUPS = ((0, 1, 2),)
BF = jnp.bfloat16
F32 = jnp.float32


def codes(master, width):
    capped = jnp.minimum(jnp.maximum(master.astype(F32), -128.0), 127.5)
    if width == 0:
        return jnp.floor(capped).astype(BF)
    step = 16.0 if width == 1 else 64.0
    return (jnp.floor(capped * (1.0 / step)) + 0.5).astype(BF)


STEP = (1.0, 16.0, 64.0)


def dot_rows(left, right):
    return lax.dot_general(left, right, (((1,), (1,)), ((), ())), preferred_element_type=F32)


def dot_cols(left, right):
    return lax.dot_general(left, right, (((0,), (0,)), ((), ())), preferred_element_type=F32)


def dot(left, right):
    return lax.dot_general(left, right, (((1,), (0,)), ((), ())), preferred_element_type=F32)


def inverse_rms(value):
    return lax.rsqrt(jnp.mean(value * value, axis=-1, keepdims=True) + 1e-06)


def rms_back(value, inverse, gain, grad):
    scaled = value * inverse
    gain_grad = jnp.sum(grad * scaled, axis=0, keepdims=True)
    weighted = grad * gain
    mean = jnp.mean(weighted * scaled, axis=-1, keepdims=True)
    return inverse * (weighted - scaled * mean), gain_grad


def doc_info(positions, doc_lengths):
    slots = jnp.arange(doc_lengths.shape[0], dtype=jnp.int32)
    ends = jnp.sum(jnp.where(slots[:, None] <= slots[None, :], doc_lengths[:, None], 0), axis=0)
    before = ends[None, :] <= positions[:, None]
    segment = jnp.sum(before.astype(jnp.int32), axis=1)
    offset = jnp.sum(jnp.where(before, doc_lengths[None, :], 0), axis=1)
    return segment, positions - offset


def rotate(value, cosine, sine):
    half = value.shape[-1] // 2
    first, second = value[:, :half], value[:, half:]
    return jnp.concatenate([first * cosine - second * sine, second * cosine + first * sine], axis=1)


def gelu_parts(gate):
    root = math.sqrt(2.0 / math.pi)
    square = gate * gate
    bend = jnp.tanh(root * gate * (1.0 + 0.044715 * square))
    half = 0.5 * (1.0 + bend)
    slope = half + 0.5 * gate * (1.0 - bend * bend) * root * (1.0 + 3.0 * 0.044715 * square)
    return gate * half, slope


def make_body(seq_size):
    line = seq_size // 2
    core_pairs = [(i, i ^ 1) for i in range(4)]
    far_pairs = [(i, i ^ 2) for i in range(4)]
    side_pairs = [(i, i ^ 1) for i in range(seq_size)]

    def core_swap(value):
        return lax.ppermute(value, "head", core_pairs)

    def far_swap(value):
        return lax.ppermute(value, "head", far_pairs)

    def side_swap(value):
        return lax.ppermute(value, "seq", side_pairs)

    def line_shift(value, hops):
        pairs = [(i, i + 2 * hops) for i in range(seq_size) if 0 <= i + 2 * hops < seq_size]
        return lax.ppermute(value, "seq", pairs)

    def line_turn(value, hops):
        return lax.ppermute(value, "seq", [(i, (i + 2 * hops) % seq_size) for i in range(seq_size)])

    def reduce_head(part):
        count, rows, width = part.shape
        half, quarter = rows // 2, rows // 4
        got = core_swap(part[:, half:].astype(BF))
        both = part[:, :half] + got.astype(F32)
        got = far_swap(both[:, quarter:].astype(BF))
        return both[:, :quarter] + got.astype(F32)

    def gather_head(own):
        two = jnp.concatenate([own, far_swap(own)], axis=1)
        return jnp.concatenate([two, core_swap(two)], axis=1)

    def line_scatter(chunks, place):
        def pick(index):
            return lax.dynamic_index_in_dim(chunks, jnp.clip(index, 0, line - 1), 0, keepdims=False)

        up = down = None
        for step in range(1, line):
            ahead, behind = pick(place + line - step), pick(place - line + step)
            up = line_shift((ahead if up is None else ahead + up.astype(F32)).astype(BF), 1)
            down = line_shift((behind if down is None else behind + down.astype(F32)).astype(BF), -1)
        return pick(place) + up.astype(F32) + down.astype(F32)

    def body(
        tokens, cotangent, doc_lengths, pad_mask, gain_one, gain_two, gain_three, gain_four,
        w_query, w_key, w_value, w_out, w_gate, w_up, w_down,
    ):
        rows, width = tokens.shape
        quarter = rows // 4
        heads = w_query.shape[0] // HD
        hidden = w_gate.shape[0]
        head_all, hidden_all = 4 * w_query.shape[0], 4 * hidden
        sm = 1.0 / (64.0 * math.sqrt(width))
        so = 1.0 / (64.0 * math.sqrt(head_all))
        sf = 1.0 / (64.0 * math.sqrt(hidden_all))
        root_scale = 1.0 / math.sqrt(HD)
        h, s = lax.axis_index("head"), lax.axis_index("seq")
        place, side = s // 2, s % 2
        orders = [h, h ^ 2, h ^ 1, h ^ 3]

        def relative(value):
            return jnp.concatenate(
                [lax.dynamic_slice_in_dim(value, o * quarter, quarter, 0) for o in orders], axis=0
            )

        def natural(value):
            parts = []
            for block in range(4):
                bits = h ^ block
                slot = (bits % 2) * 2 + bits // 2
                parts.append(lax.dynamic_slice_in_dim(value, slot * quarter, quarter, 1))
            return jnp.concatenate(parts, axis=1)

        def halves(master):
            parts = master.reshape(line, 2, hidden // seq_size, width)
            return jnp.concatenate(
                [
                    lax.dynamic_index_in_dim(parts, which, 1, keepdims=False).reshape(hidden // 2, width)
                    for which in (side, 1 - side)
                ],
                axis=0,
            )

        x_all = relative(tokens).astype(F32)
        x_own = x_all[:quarter]
        dy_own = lax.dynamic_slice_in_dim(cotangent, h * quarter, quarter, 1)
        within = jnp.concatenate(
            [o * quarter + jnp.arange(quarter, dtype=jnp.int32) for o in orders], axis=0
        )
        position = s * rows + within
        segment, turn = doc_info(position, doc_lengths)
        freq = jnp.exp(jnp.arange(HD // 2, dtype=F32) * (-2.0 * math.log(10000.0) / HD))
        angle = turn.astype(F32)[:, None] * freq[None, :]
        cosine, sine = jnp.cos(angle), jnp.sin(angle)

        inverse_one = inverse_rms(x_all)
        n1 = (x_all * inverse_one * gain_one).astype(BF)
        master_qkv = jnp.concatenate([w_query, w_key, w_value], axis=0)
        gate_rows, up_rows, down_rows = halves(w_gate), halves(w_up), halves(w_down)

        queries, blocks = [], []
        for w in range(3):
            qkv = dot_rows(n1, codes(master_qkv, w)) * (sm * STEP[w])
            queries.append(
                jnp.concatenate(
                    [rotate(qkv[:, j * HD : (j + 1) * HD], cosine, sine) for j in range(heads)], axis=0
                ).astype(BF)
            )
            key = rotate(qkv[:, heads * HD : (heads + 1) * HD], cosine, sine)
            blocks.append(jnp.concatenate([key, qkv[:, (heads + 1) * HD :]], axis=1).astype(BF))
        pad_row = relative(pad_mask).astype(BF)[None, :]
        pad_block = jnp.pad(pad_row, ((0, 15), (0, 2 * HD - rows)))
        packed = jnp.concatenate(blocks + [pad_block], axis=0)
        near = [packed] + [line_shift(packed, hops) for hops in range(1, line)]
        across = [side_swap(block) for block in near]
        pieces, key_position = [], []
        for hops in range(line):
            for which, block in ((side, near[hops]), (1 - side, across[hops])):
                pieces.append(block)
                key_position.append((2 * (place - hops) + which) * rows + within)
        key_position = jnp.concatenate(key_position, axis=0)
        key_valid = jnp.concatenate([b[3 * rows, :rows] for b in pieces], axis=0) > 0.5
        key_segment, _ = doc_info(key_position, doc_lengths)
        allowed = (
            (segment[:, None] == key_segment[None, :])
            & (key_position[None, :] <= position[:, None])
            & (key_position[None, :] >= 0)
            & (key_valid[None, :] | (key_position[None, :] == position[:, None]))
        )
        allowed = jnp.concatenate([allowed] * heads, axis=0)
        n1_all = lax.all_gather(n1, "seq", axis=0, tiled=True)

        keys, values, probs, slopes, contexts, part_attn = [], [], [], [], [], []
        for w in range(3):
            key = jnp.concatenate([b[w * rows : (w + 1) * rows, :HD] for b in pieces], axis=0)
            value = jnp.concatenate([b[w * rows : (w + 1) * rows, HD:] for b in pieces], axis=0)
            bend = jnp.tanh(dot_rows(queries[w], key) * (root_scale / SOFTCAP))
            expo = jnp.where(allowed, jnp.exp(SOFTCAP * bend), 0.0)
            weight = expo / jnp.sum(expo, axis=1, keepdims=True)
            prob = weight.astype(BF)
            slope = (weight * (1.0 - bend * bend) * root_scale).astype(BF)
            context = dot(prob, value).astype(BF)
            context = jnp.concatenate(
                [context[j * rows : (j + 1) * rows] for j in range(heads)], axis=1
            )
            keys.append(key)
            values.append(value)
            probs.append(prob)
            slopes.append(slope)
            contexts.append(context)
            part_attn.append(dot(context, codes(w_out, w)) * (so * STEP[w]))

        def of(items, group):
            return jnp.stack([items[w] for w in group])

        gain_sums = [jnp.zeros((1, width), F32)] * 4
        out_own, middle_grads = [None] * 3, jnp.zeros((quarter, width), F32)
        d_attns = [None] * 3
        left_down, right_down, left_gate, left_up, right_gate = [], [], [], [], []
        for group in GROUPS:
            n = len(group)
            attn = reduce_head(of(part_attn, group))
            inverse_two = inverse_rms(attn)
            middle = x_own + attn * inverse_two * gain_two
            inverse_three = inverse_rms(middle)
            n2_own = (middle * inverse_three * gain_three).astype(BF)
            n2 = gather_head(n2_own)
            hids, slopes_gate, slopes_up, part_ff = [], [], [], []
            for i, w in enumerate(group):
                gate = dot_rows(n2[i], codes(gate_rows, w)) * (sm * STEP[w])
                up = dot_rows(n2[i], codes(up_rows, w)) * (sm * STEP[w])
                act, slope = gelu_parts(gate)
                hid = (act * up).astype(BF)
                hids.append(hid)
                slopes_gate.append((up * slope).astype(BF))
                slopes_up.append(act.astype(BF))
                part_ff.append(dot(hid, codes(down_rows, w)) * (sf * STEP[w]))
            ff = reduce_head(jnp.stack(part_ff))
            inverse_four = inverse_rms(ff)
            dy = of(dy_own, group).astype(F32)
            result = (middle + ff * inverse_four * gain_four).astype(BF)
            d_ff_own, sums = rms_back(
                ff.reshape(n * quarter, width), inverse_four.reshape(n * quarter, 1), gain_four,
                dy.reshape(n * quarter, width),
            )
            gain_sums[3] = gain_sums[3] + sums
            d_ff = gather_head(d_ff_own.astype(BF).reshape(n, quarter, width))
            d_gates, d_ups, part_n2 = [], [], []
            for i, w in enumerate(group):
                d_hid = (dot_rows(d_ff[i], codes(down_rows, w)) * (sf * STEP[w])).astype(BF).astype(F32)
                d_gate = (d_hid * slopes_gate[i].astype(F32)).astype(BF)
                d_up = (d_hid * slopes_up[i].astype(F32)).astype(BF)
                d_gates.append(d_gate)
                d_ups.append(d_up)
                part_n2.append(
                    (dot(d_gate, codes(gate_rows, w)) + dot(d_up, codes(up_rows, w))) * (sm * STEP[w])
                )
            d_n2 = reduce_head(jnp.stack(part_n2)).reshape(n * quarter, width)
            d_norm, sums = rms_back(
                middle.reshape(n * quarter, width), inverse_three.reshape(n * quarter, 1), gain_three, d_n2
            )
            gain_sums[2] = gain_sums[2] + sums
            d_middle = dy.reshape(n * quarter, width) + d_norm
            d_attn_own, sums = rms_back(
                attn.reshape(n * quarter, width), inverse_two.reshape(n * quarter, 1), gain_two, d_middle
            )
            gain_sums[1] = gain_sums[1] + sums
            middle_grads = middle_grads + jnp.sum(d_middle.reshape(n, quarter, width), axis=0)
            d_attn = gather_head(d_attn_own.astype(BF).reshape(n, quarter, width))
            for i, w in enumerate(group):
                out_own[w] = result[i]
                d_attns[w] = d_attn[i]
            half_rows = rows // 2

            def both_sides(value):
                got = side_swap(value[:, :half_rows])
                got = jnp.concatenate([got, core_swap(got)], axis=1)
                return [value.reshape(n * rows, width), got.reshape(n * rows, width)]

            def both_halves(items):
                item = jnp.concatenate(items, axis=0)
                return [item[:, : hidden // 2], side_swap(item[:, hidden // 2 :])]

            right_gate += both_sides(n2)
            left_down += both_halves(hids)
            right_down += both_sides(d_ff)
            left_gate += both_halves(d_gates)
            left_up += both_halves(d_ups)

        activations = natural(gather_head(jnp.stack(out_own)))
        owned = hidden // seq_size

        def weight_grad(left, right, scale):
            total = dot_cols(jnp.concatenate(left, axis=0), jnp.concatenate(right, axis=0)) * scale
            return line_scatter(total.reshape(line, owned, width), place)

        grad_down = weight_grad(left_down, right_down, sf)
        grad_gate = weight_grad(left_gate, right_gate, sm)
        grad_up = weight_grad(left_up, right_gate, sm)

        d_qs, d_blocks = [], []
        for w in range(3):
            d_context = (dot_rows(d_attns[w], codes(w_out, w)) * (so * STEP[w])).astype(BF)
            d_context = jnp.concatenate(
                [d_context[:, j * HD : (j + 1) * HD] for j in range(heads)], axis=0
            )
            d_prob = dot_rows(d_context, values[w])
            delta = jnp.sum(probs[w].astype(F32) * d_prob, axis=1, keepdims=True)
            d_score = (slopes[w].astype(F32) * (d_prob - delta)).astype(BF)
            d_q = dot(d_score, keys[w]).astype(BF).astype(F32)
            d_qs.append(
                jnp.concatenate(
                    [rotate(d_q[j * rows : (j + 1) * rows], cosine, -sine) for j in range(heads)], axis=1
                ).astype(BF)
            )
            d_key = dot_cols(d_score, queries[w])
            d_value = dot_cols(probs[w], d_context)
            d_blocks.append(
                jnp.concatenate([d_key, d_value], axis=1).reshape(line, 2, rows, 2 * HD)
            )
        d_block = jnp.stack(d_blocks, axis=1)
        got = side_swap(d_block[:, :, 1].astype(BF))
        d_block = d_block[:, :, 0] + got.astype(F32)
        d_kv = d_block[0]
        for hops in range(1, line):
            d_kv = d_kv + line_shift(d_block[hops].astype(BF), -hops).astype(F32)
        d_qkv = []
        part_n1 = jnp.zeros((rows, width), F32)
        for w in range(3):
            d_key = d_kv[w, :, :HD].astype(BF).astype(F32)
            d_qkv.append(
                jnp.concatenate(
                    [d_qs[w], rotate(d_key, cosine, -sine).astype(BF), d_kv[w, :, HD:].astype(BF)], axis=1
                )
            )
            part_n1 = part_n1 + dot(d_qkv[w], codes(master_qkv, w)) * (sm * STEP[w])
        d_n1 = reduce_head(part_n1[None])[0]
        d_norm, sums = rms_back(x_own, inverse_one[:quarter], gain_one, d_n1)
        gain_sums[0] = sums
        grad_tokens = natural(gather_head((middle_grads + d_norm).astype(BF)[None]))[0]

        owned_out = w_out.shape[0] // seq_size
        term = dot_cols(jnp.concatenate(contexts, axis=0), jnp.concatenate(d_attns, axis=0)) * so
        term = term.reshape(line, 2, owned_out, width)
        got = side_swap(lax.dynamic_index_in_dim(term, 1 - side, 1, keepdims=False).astype(BF))
        term = lax.dynamic_index_in_dim(term, side, 1, keepdims=False) + got.astype(F32)
        grad_out = line_scatter(term, place)

        d_sum = (d_qkv[0].astype(F32) + d_qkv[1].astype(F32) + d_qkv[2].astype(F32)).astype(BF).T
        cuts = [w_query.shape[0], w_key.shape[0], w_value.shape[0]]
        sent, begin = [], 0
        for cut in cuts:
            sent.append(d_sum[begin : begin + cut].reshape(seq_size, cut // seq_size, rows))
            begin += cut
        sent = jnp.concatenate(sent, axis=1)
        owned_qkv = sent.shape[1]
        sent = sent.reshape(line, 2, owned_qkv, rows)
        other = side_swap(lax.dynamic_index_in_dim(sent, 1 - side, 1, keepdims=False))
        own = lax.dynamic_index_in_dim(sent, side, 1, keepdims=False)
        both = jnp.stack([own, other], axis=1)
        n1_line = n1_all.reshape(line, 2, rows, width)
        total = jnp.zeros((owned_qkv, width), F32)
        for hops in range(line):
            chunk = lax.dynamic_index_in_dim(both, (place + hops) % line, 0, keepdims=False)
            if hops:
                chunk = line_turn(chunk, hops)
            source = lax.dynamic_index_in_dim(n1_line, (place - hops) % line, 0, keepdims=False)
            for slot, which in ((0, side), (1, 1 - side)):
                total = total + dot(chunk[slot], lax.dynamic_index_in_dim(source, which, 0, keepdims=False))
        total = total * sm
        cut_q, cut_k = cuts[0] // seq_size, cuts[1] // seq_size
        grad_query, grad_key, grad_value = (
            total[:cut_q], total[cut_q : cut_q + cut_k], total[cut_q + cut_k :],
        )

        sums = jnp.concatenate(gain_sums, axis=0)
        sums = sums + core_swap(sums)
        sums = sums + far_swap(sums)
        bit = 1
        while bit < seq_size:
            sums = sums + lax.ppermute(sums, "seq", [(i, i ^ bit) for i in range(seq_size)])
            bit *= 2
        share = width // seq_size
        sums = lax.dynamic_slice_in_dim(sums, s * share, share, 1)
        return (
            activations, grad_tokens, grad_query, grad_key, grad_value, grad_out, grad_gate, grad_up,
            grad_down, sums[0], sums[1], sums[2], sums[3],
        )

    return body


def solution(mesh):
    row, rep, vec = P("head", None), P(), P("seq")
    in_specs = (P("seq", None), P(None, "seq", None), rep, vec, rep, rep, rep, rep) + (row,) * 7
    both = P(("head", "seq"), None)
    out_specs = (P(None, "seq", None), P("seq", None)) + (both,) * 7 + (vec,) * 4
    return jax.shard_map(
        make_body(mesh.shape["seq"]), mesh=mesh, in_specs=in_specs, out_specs=out_specs, check_vma=False
    )
```

```python
import functools
import math

import jax
import jax.numpy as jnp
from jax import lax
from jax.experimental import pallas as pl
from jax.experimental.pallas import tpu as pltpu
from jax.sharding import PartitionSpec as P

HD = 256
SOFTCAP = 50.0
WIDTHS = (8, 4, 2)
BF = jnp.bfloat16
F32 = jnp.float32


def codes(master, width):
    capped = jnp.minimum(jnp.maximum(master.astype(F32), -128.0), 127.5)
    if width == 0:
        return jnp.floor(capped).astype(BF)
    step = 16.0 if width == 1 else 64.0
    return (jnp.floor(capped * (1.0 / step)) + 0.5).astype(BF)


STEP = (1.0, 16.0, 64.0)


def dot_rows(left, right):
    return lax.dot_general(left, right, (((1,), (1,)), ((), ())), preferred_element_type=F32)


def dot_cols(left, right):
    return lax.dot_general(left, right, (((0,), (0,)), ((), ())), preferred_element_type=F32)


def dot(left, right):
    return lax.dot_general(left, right, (((1,), (0,)), ((), ())), preferred_element_type=F32)


def inverse_rms(value):
    return lax.rsqrt(jnp.mean(value * value, axis=-1, keepdims=True) + 1e-06)


def rms_back(value, inverse, gain, grad):
    scaled = value * inverse
    gain_grad = jnp.sum(grad * scaled, axis=0, keepdims=True)
    weighted = grad * gain
    mean = jnp.mean(weighted * scaled, axis=-1, keepdims=True)
    return inverse * (weighted - scaled * mean), gain_grad


def doc_info(positions, doc_lengths):
    slots = jnp.arange(doc_lengths.shape[0], dtype=jnp.int32)
    ends = jnp.sum(jnp.where(slots[:, None] <= slots[None, :], doc_lengths[:, None], 0), axis=0)
    before = ends[None, :] <= positions[:, None]
    segment = jnp.sum(before.astype(jnp.int32), axis=1)
    offset = jnp.sum(jnp.where(before, doc_lengths[None, :], 0), axis=1)
    return segment, positions - offset


def rotate(value, cosine, sine):
    half = value.shape[-1] // 2
    first, second = value[:, :half], value[:, half:]
    return jnp.concatenate([first * cosine - second * sine, second * cosine + first * sine], axis=1)


def gelu_parts(gate):
    root = math.sqrt(2.0 / math.pi)
    square = gate * gate
    bend = jnp.tanh(root * gate * (1.0 + 0.044715 * square))
    half = 0.5 * (1.0 + bend)
    slope = half + 0.5 * gate * (1.0 - bend * bend) * root * (1.0 + 3.0 * 0.044715 * square)
    return gate * half, slope


def all_codes(master):
    capped = jnp.minimum(jnp.maximum(master.astype(F32), -128.0), 127.5)
    return [
        jnp.floor(capped).astype(BF),
        (jnp.floor(capped * (1.0 / STEP[1])) + 0.5).astype(BF),
        (jnp.floor(capped * (1.0 / STEP[2])) + 0.5).astype(BF),
    ]


PARTS = 3
VMEM = 60 * 2**20


def hidden_call(kernel, side, acts, tiles, weights, out_count, cost):
    line, _, owned, width = weights[0].shape
    rows = acts[0].shape[1]
    piece = owned // PARTS
    block = line * piece
    whole = [pl.BlockSpec(a.shape, lambda j, s: (0, 0, 0)) for a in acts]
    tile = pl.BlockSpec((3, rows, block), lambda j, s: (0, 0, j))
    weight = pl.BlockSpec(
        (line, 1, piece, width), lambda j, s: (0, jnp.where(j < PARTS, s[0], 1 - s[0]), j % PARTS, 0)
    )
    return pl.pallas_call(
        kernel,
        grid_spec=pltpu.PrefetchScalarGridSpec(
            num_scalar_prefetch=1,
            grid=(2 * PARTS,),
            in_specs=whole + [tile] * len(tiles) + [weight] * len(weights),
            out_specs=[tile] * out_count,
        ),
        out_shape=[jax.ShapeDtypeStruct((3, rows, 2 * line * owned), BF)] * out_count,
        compiler_params=pltpu.CompilerParams(vmem_limit_bytes=VMEM),
        cost_estimate=pl.CostEstimate(flops=cost, bytes_accessed=cost // 400, transcendentals=0),
    )(side, *acts, *tiles, *weights)


def model_call(kernel, side, acts, weights, block, cost):
    line, _, owned, width = weights[0].shape
    rows = acts[0].shape[1]
    whole = [pl.BlockSpec(a.shape, lambda j, s: (0, 0, 0)) for a in acts]
    weight = pl.BlockSpec((line, 2, owned, block), lambda j, s: (0, 0, 0, j))
    out = pl.BlockSpec((3, rows // 2, block), lambda j, s: (0, 0, j))
    return pl.pallas_call(
        kernel,
        grid_spec=pltpu.PrefetchScalarGridSpec(
            num_scalar_prefetch=1,
            grid=(width // block,),
            in_specs=whole + [weight] * len(weights),
            out_specs=[out, out],
        ),
        out_shape=[jax.ShapeDtypeStruct((3, rows // 2, width), BF)] * 2,
        compiler_params=pltpu.CompilerParams(vmem_limit_bytes=VMEM),
        cost_estimate=pl.CostEstimate(flops=cost, bytes_accessed=cost // 400, transcendentals=0),
    )(side, *acts, *weights)


def weight_rows(ref):
    line, _, piece, width = ref.shape
    return ref[...].reshape(line * piece, width)


def weight_columns(side, ref):
    line, _, owned, _ = ref.shape
    piece = owned // PARTS
    return jnp.concatenate(
        [
            ref[place, which, part * piece : (part + 1) * piece, :]
            for which in (side, 1 - side)
            for part in range(PARTS)
            for place in range(line)
        ],
        axis=0,
    )


def gate_up_kernel(scale, side_ref, n2_ref, gate_ref, up_ref, hid_ref, slope_gate_ref, slope_up_ref):
    gates, ups = all_codes(weight_rows(gate_ref)), all_codes(weight_rows(up_ref))
    for w in range(3):
        n2 = n2_ref[w]
        gate = dot_rows(n2, gates[w]) * (scale * STEP[w])
        up = dot_rows(n2, ups[w]) * (scale * STEP[w])
        act, slope = gelu_parts(gate)
        hid_ref[w] = (act * up).astype(BF)
        slope_gate_ref[w] = (up * slope).astype(BF)
        slope_up_ref[w] = act.astype(BF)


def down_kernel(scale, side_ref, hid_ref, down_ref, first_ref, second_ref):
    half = first_ref.shape[1]
    for w, code in enumerate(all_codes(weight_columns(side_ref[0], down_ref))):
        part = (dot(hid_ref[w], code) * (scale * STEP[w])).astype(BF)
        first_ref[w] = part[:half]
        second_ref[w] = part[half:]


def d_hidden_kernel(scale, side_ref, d_ff_ref, slope_gate_ref, slope_up_ref, down_ref, d_gate_ref, d_up_ref):
    for w, code in enumerate(all_codes(weight_rows(down_ref))):
        d_hid = (dot_rows(d_ff_ref[w], code) * (scale * STEP[w])).astype(BF).astype(F32)
        d_gate_ref[w] = (d_hid * slope_gate_ref[w].astype(F32)).astype(BF)
        d_up_ref[w] = (d_hid * slope_up_ref[w].astype(F32)).astype(BF)


def d_model_kernel(scale, side_ref, d_gate_ref, d_up_ref, gate_ref, up_ref, first_ref, second_ref):
    half = first_ref.shape[1]
    gates = all_codes(weight_columns(side_ref[0], gate_ref))
    ups = all_codes(weight_columns(side_ref[0], up_ref))
    for w in range(3):
        part = dot(d_gate_ref[w], gates[w]) + dot(d_up_ref[w], ups[w])
        part = (part * (scale * STEP[w])).astype(BF)
        first_ref[w] = part[:half]
        second_ref[w] = part[half:]


def make_body(seq_size):
    line = seq_size // 2
    core_pairs = [(i, i ^ 1) for i in range(4)]
    far_pairs = [(i, i ^ 2) for i in range(4)]
    side_pairs = [(i, i ^ 1) for i in range(seq_size)]

    def core_swap(value):
        return lax.ppermute(value, "head", core_pairs)

    def far_swap(value):
        return lax.ppermute(value, "head", far_pairs)

    def side_swap(value):
        return lax.ppermute(value, "seq", side_pairs)

    def line_shift(value, hops):
        pairs = [(i, i + 2 * hops) for i in range(seq_size) if 0 <= i + 2 * hops < seq_size]
        return lax.ppermute(value, "seq", pairs)

    def line_turn(value, hops):
        return lax.ppermute(value, "seq", [(i, (i + 2 * hops) % seq_size) for i in range(seq_size)])

    def reduce_head(part):
        half = part.shape[1] // 2
        return reduce_halves(part[:, :half], part[:, half:].astype(BF))

    def reduce_halves(kept, sent):
        quarter = kept.shape[1] // 2
        both = kept.astype(F32) + core_swap(sent).astype(F32)
        got = far_swap(both[:, quarter:].astype(BF))
        return both[:, :quarter] + got.astype(F32)

    def gather_head(own):
        two = jnp.concatenate([own, far_swap(own)], axis=1)
        return jnp.concatenate([two, core_swap(two)], axis=1)

    lines = [list(range(first, seq_size, 2)) for first in range(2)]

    def line_scatter(chunks):
        return lax.psum_scatter(
            chunks, "seq", scatter_dimension=0, axis_index_groups=lines, tiled=True
        ).astype(F32)

    def body(
        tokens, cotangent, doc_lengths, pad_mask, gain_one, gain_two, gain_three, gain_four,
        w_query, w_key, w_value, w_out, w_gate, w_up, w_down,
    ):
        rows, width = tokens.shape
        quarter = rows // 4
        heads = w_query.shape[0] // HD
        hidden = w_gate.shape[0]
        head_all, hidden_all = 4 * w_query.shape[0], 4 * hidden
        sm = 1.0 / (64.0 * math.sqrt(width))
        so = 1.0 / (64.0 * math.sqrt(head_all))
        sf = 1.0 / (64.0 * math.sqrt(hidden_all))
        root_scale = 1.0 / math.sqrt(HD)
        h, s = lax.axis_index("head"), lax.axis_index("seq")
        place, side = s // 2, s % 2
        orders = [h, h ^ 2, h ^ 1, h ^ 3]

        def relative(value):
            return jnp.concatenate(
                [lax.dynamic_slice_in_dim(value, o * quarter, quarter, 0) for o in orders], axis=0
            )

        def natural(value):
            parts = []
            for block in range(4):
                bits = h ^ block
                slot = (bits % 2) * 2 + bits // 2
                parts.append(lax.dynamic_slice_in_dim(value, slot * quarter, quarter, 1))
            return jnp.concatenate(parts, axis=1)

        x_all = relative(tokens).astype(F32)
        x_own = x_all[:quarter]
        dy_own = lax.dynamic_slice_in_dim(cotangent, h * quarter, quarter, 1)
        within = jnp.concatenate(
            [o * quarter + jnp.arange(quarter, dtype=jnp.int32) for o in orders], axis=0
        )
        position = s * rows + within
        segment, turn = doc_info(position, doc_lengths)
        freq = jnp.exp(jnp.arange(HD // 2, dtype=F32) * (-2.0 * math.log(10000.0) / HD))
        angle = turn.astype(F32)[:, None] * freq[None, :]
        cosine, sine = jnp.cos(angle), jnp.sin(angle)

        inverse_one = inverse_rms(x_all)
        n1 = (x_all * inverse_one * gain_one).astype(BF)
        master_qkv = jnp.concatenate([w_query, w_key, w_value], axis=0)
        gate_rows, up_rows, down_rows = (
            w.reshape(line, 2, hidden // seq_size, width) for w in (w_gate, w_up, w_down)
        )
        which_side = jnp.reshape(side, (1,)).astype(jnp.int32)

        half_rows = rows // 2
        pad_row = relative(pad_mask).astype(BF)[None, :]
        pad_block = jnp.pad(pad_row, ((0, 15), (0, width - rows)))
        packed = jnp.concatenate([n1[:half_rows], pad_block], axis=0)
        near = [packed] + [line_turn(packed, hops) for hops in range(1, line)]
        pieces, valid, key_position = [], [], []
        for hops in range(line):
            pair = [near[hops], side_swap(near[hops])]
            other = core_swap(jnp.concatenate([b[:half_rows] for b in pair], axis=0))
            for slot, which in ((0, side), (1, 1 - side)):
                pieces += [pair[slot][:half_rows], other[slot * half_rows : (slot + 1) * half_rows]]
                valid.append(pair[slot][half_rows, :rows])
                key_position.append((2 * ((place - hops) % line) + which) * rows + within)
        n1_all = jnp.concatenate(pieces, axis=0)
        key_position = jnp.concatenate(key_position, axis=0)
        key_valid = jnp.concatenate(valid, axis=0) > 0.5
        key_segment, key_turn = doc_info(key_position, doc_lengths)
        key_angle = key_turn.astype(F32)[:, None] * freq[None, :]
        key_cosine, key_sine = jnp.cos(key_angle), jnp.sin(key_angle)
        allowed = (
            (segment[:, None] == key_segment[None, :])
            & (key_position[None, :] <= position[:, None])
            & (key_valid[None, :] | (key_position[None, :] == position[:, None]))
        )
        allowed = jnp.concatenate([allowed] * heads, axis=0)
        master_kv = jnp.concatenate([w_key, w_value], axis=0)

        queries, keys, values, probs, slopes, contexts, part_attn = [], [], [], [], [], [], []
        for w in range(3):
            query = dot_rows(n1, codes(w_query, w)) * (sm * STEP[w])
            queries.append(
                jnp.concatenate(
                    [rotate(query[:, j * HD : (j + 1) * HD], cosine, sine) for j in range(heads)], axis=0
                ).astype(BF)
            )
            kv = dot_rows(n1_all, codes(master_kv, w)) * (sm * STEP[w])
            key = rotate(kv[:, :HD], key_cosine, key_sine).astype(BF)
            value = kv[:, HD:].astype(BF)
            bend = jnp.tanh(dot_rows(queries[w], key) * (root_scale / SOFTCAP))
            expo = jnp.where(allowed, jnp.exp(SOFTCAP * bend), 0.0)
            weight = expo / jnp.sum(expo, axis=1, keepdims=True)
            prob = weight.astype(BF)
            slope = (weight * (1.0 - bend * bend) * root_scale).astype(BF)
            context = dot(prob, value).astype(BF)
            context = jnp.concatenate(
                [context[j * rows : (j + 1) * rows] for j in range(heads)], axis=1
            )
            keys.append(key)
            values.append(value)
            probs.append(prob)
            slopes.append(slope)
            contexts.append(context)
            part_attn.append(dot(context, codes(w_out, w)) * (so * STEP[w]))

        def flat(value):
            return value.reshape(3 * value.shape[1], value.shape[2])

        def both_sides(value):
            got = side_swap(value[:, :half_rows])
            return jnp.concatenate([flat(value), flat(jnp.concatenate([got, core_swap(got)], axis=1))], axis=0)

        def both_halves(value):
            value = flat(value)
            return jnp.concatenate(
                [value[:, : hidden // 2], side_swap(value[:, hidden // 2 :])], axis=0
            )

        def weight_grad(left, right, scale):
            total = (dot_cols(left, right) * scale).astype(BF)
            owned = hidden // seq_size
            total = total.reshape(PARTS, line, owned // PARTS, width).swapaxes(0, 1)
            return line_scatter(total.reshape(line * owned, width))

        attn = reduce_head(jnp.stack(part_attn))
        inverse_two = inverse_rms(attn)
        middle = x_own + attn * inverse_two * gain_two
        inverse_three = inverse_rms(middle)
        n2 = gather_head((middle * inverse_three * gain_three).astype(BF))
        cost = 6 * rows * hidden * width
        hid, slope_gate, slope_up = hidden_call(
            functools.partial(gate_up_kernel, sm), which_side, [n2], [], [gate_rows, up_rows], 3, 2 * cost
        )
        right_gate = both_sides(n2)
        ff = reduce_halves(
            *model_call(functools.partial(down_kernel, sf), which_side, [hid], [down_rows], 384, cost)
        )
        left_down = both_halves(hid)
        inverse_four = inverse_rms(ff)
        dy = dy_own.astype(F32)
        result = (middle + ff * inverse_four * gain_four).astype(BF)
        d_ff_own, sums_four = rms_back(flat(ff), flat(inverse_four), gain_four, flat(dy))
        d_ff = gather_head(d_ff_own.astype(BF).reshape(3, quarter, width))
        right_down = both_sides(d_ff)
        d_gate, d_up = hidden_call(
            functools.partial(d_hidden_kernel, sf), which_side, [d_ff], [slope_gate, slope_up],
            [down_rows], 2, cost,
        )
        grad_down = weight_grad(left_down, right_down, sf)
        d_n2 = flat(
            reduce_halves(
                *model_call(
                    functools.partial(d_model_kernel, sm), which_side, [d_gate, d_up],
                    [gate_rows, up_rows], 384, 2 * cost,
                )
            )
        )
        left_gate, left_up = both_halves(d_gate), both_halves(d_up)
        grad_gate = weight_grad(left_gate, right_gate, sm)
        grad_up = weight_grad(left_up, right_gate, sm)
        d_norm, sums_three = rms_back(flat(middle), flat(inverse_three), gain_three, d_n2)
        d_middle = flat(dy) + d_norm
        d_attn_own, sums_two = rms_back(flat(attn), flat(inverse_two), gain_two, d_middle)
        middle_grads = jnp.sum(d_middle.reshape(3, quarter, width), axis=0)
        d_attns = gather_head(d_attn_own.astype(BF).reshape(3, quarter, width))
        activations = natural(gather_head(result))

        d_qs, d_blocks = [], []
        for w in range(3):
            d_context = (dot_rows(d_attns[w], codes(w_out, w)) * (so * STEP[w])).astype(BF)
            d_context = jnp.concatenate(
                [d_context[:, j * HD : (j + 1) * HD] for j in range(heads)], axis=0
            )
            d_prob = dot_rows(d_context, values[w])
            delta = jnp.sum(probs[w].astype(F32) * d_prob, axis=1, keepdims=True)
            d_score = (slopes[w].astype(F32) * (d_prob - delta)).astype(BF)
            d_q = dot(d_score, keys[w]).astype(BF).astype(F32)
            d_qs.append(
                jnp.concatenate(
                    [rotate(d_q[j * rows : (j + 1) * rows], cosine, -sine) for j in range(heads)], axis=1
                ).astype(BF)
            )
            d_key = dot_cols(d_score, queries[w])
            d_value = dot_cols(probs[w], d_context)
            d_blocks.append(
                jnp.concatenate([d_key, d_value], axis=1).reshape(line, 2, rows, 2 * HD)
            )
        d_block = jnp.stack(d_blocks, axis=1)
        got = side_swap(d_block[:, :, 1].astype(BF))
        d_block = d_block[:, :, 0] + got.astype(F32)
        d_kv = d_block[0]
        for hops in range(1, line):
            d_kv = d_kv + line_shift(d_block[hops].astype(BF), -hops).astype(F32)
        d_qkv = []
        part_n1 = jnp.zeros((rows, width), F32)
        for w in range(3):
            d_key = d_kv[w, :, :HD].astype(BF).astype(F32)
            d_qkv.append(
                jnp.concatenate(
                    [d_qs[w], rotate(d_key, cosine, -sine).astype(BF), d_kv[w, :, HD:].astype(BF)], axis=1
                )
            )
            part_n1 = part_n1 + dot(d_qkv[w], codes(master_qkv, w)) * (sm * STEP[w])
        d_n1 = reduce_head(part_n1[None])[0]
        d_norm, sums_one = rms_back(x_own, inverse_one[:quarter], gain_one, d_n1)
        grad_tokens = natural(gather_head((middle_grads + d_norm).astype(BF)[None]))[0]

        owned_out = w_out.shape[0] // seq_size
        term = dot_cols(jnp.concatenate(contexts, axis=0), flat(d_attns)) * so
        term = term.reshape(line, 2, owned_out, width)
        got = side_swap(lax.dynamic_index_in_dim(term, 1 - side, 1, keepdims=False).astype(BF))
        term = lax.dynamic_index_in_dim(term, side, 1, keepdims=False) + got.astype(F32)
        grad_out = line_scatter(term.reshape(line * owned_out, width).astype(BF))

        d_sum = (d_qkv[0].astype(F32) + d_qkv[1].astype(F32) + d_qkv[2].astype(F32)).astype(BF).T
        cuts = [w_query.shape[0], w_key.shape[0], w_value.shape[0]]
        sent, begin = [], 0
        for cut in cuts:
            sent.append(d_sum[begin : begin + cut].reshape(seq_size, cut // seq_size, rows))
            begin += cut
        sent = jnp.concatenate(sent, axis=1)
        owned_qkv = sent.shape[1]
        sent = sent.swapaxes(1, 2).reshape(line, 2, rows, owned_qkv)
        other = side_swap(lax.dynamic_index_in_dim(sent, 1 - side, 1, keepdims=False))
        own = lax.dynamic_index_in_dim(sent, side, 1, keepdims=False)
        both = jnp.stack([own, other], axis=1)
        arrived = []
        for hops in range(line):
            chunk = lax.dynamic_index_in_dim(both, (place + hops) % line, 0, keepdims=False)
            chunk = line_turn(chunk, hops) if hops else chunk
            arrived.append(chunk.reshape(2 * rows, owned_qkv))
        total = dot_cols(jnp.concatenate(arrived, axis=0), n1_all)
        total = total * sm
        cut_q, cut_k = cuts[0] // seq_size, cuts[1] // seq_size
        grad_query, grad_key, grad_value = (
            total[:cut_q], total[cut_q : cut_q + cut_k], total[cut_q + cut_k :],
        )

        sums = jnp.concatenate([sums_one, sums_two, sums_three, sums_four], axis=0)
        sums = sums + core_swap(sums)
        sums = sums + far_swap(sums)
        bit = 1
        while bit < seq_size:
            sums = sums + lax.ppermute(sums, "seq", [(i, i ^ bit) for i in range(seq_size)])
            bit *= 2
        share = width // seq_size
        sums = lax.dynamic_slice_in_dim(sums, s * share, share, 1)
        return (
            activations, grad_tokens, grad_query, grad_key, grad_value, grad_out, grad_gate, grad_up,
            grad_down, sums[0], sums[1], sums[2], sums[3],
        )

    return body


def solution(mesh):
    row, rep, vec = P("head", None), P(), P("seq")
    in_specs = (P("seq", None), P(None, "seq", None), rep, vec, rep, rep, rep, rep) + (row,) * 7
    both = P(("head", "seq"), None)
    out_specs = (P(None, "seq", None), P("seq", None)) + (both,) * 7 + (vec,) * 4
    return jax.shard_map(
        make_body(mesh.shape["seq"]), mesh=mesh, in_specs=in_specs, out_specs=out_specs, check_vma=False
    )
```
